32 devices in a mesh: lon: 8 (over y, x, core), lat: 4 (over z).
Axes of the slice: x: 2, y: 2, z: 4, core: 2. Of those that a mesh axis runs over, the one named last changes fastest.
Arguments:
- u_wind: float32 [16, 2880, 512], P(None, 'lon', 'lat'), may hold values from -6 to 6
- v_wind: float32 [16, 2880, 512], P(None, 'lon', 'lat'), may hold values from -6 to 6
- height: float32 [16, 2880, 512], P(None, 'lon', 'lat'), may hold values from -6 to 6
Outputs:
- u_next: float32 [16, 2880, 512], P(None, 'lon', 'lat')
- v_next: float32 [16, 2880, 512], P(None, 'lon', 'lat')
- height_next: float32 [16, 2880, 512], P(None, 'lon', 'lat')
The draws below stay inside these ranges and needn't reach their ends.
All inputs are finite; a program needn't handle non-finite values.
Results may differ from the reference program's by a relative error of at most 0.00013.
Values sent between devices are 32-bit elements; how exact they have to be, the bound alone decides.
A program may use at most 192 MiB of HBM per device.

```python
import math
import jax
import jax.numpy as jnp

NLON = 2880
LEV = 16
NLAT = 512


def steps_of(own_key, extent, split, low, largest):
    gain = 1.0
    for position, shards_of in split:
        draws = jax.random.uniform(jax.random.fold_in(jax.random.fold_in(own_key, 6), position), (shards_of,), jnp.float32, low / len(split), largest / len(split))
        gain = gain * jnp.repeat(jnp.exp(draws), extent[position] // shards_of).reshape((-1,) + (1,) * (len(extent) - 1 - position))
    return gain


def noise(stream_key, shape, deviation, most, shards=(), held_as=jnp.bfloat16):
    level = steps_of(stream_key, shape, shards, -0.22, 0.18) if shards else 1.0
    result = jax.random.normal(stream_key, shape, jnp.float32) * deviation * level
    return jnp.minimum(jnp.maximum(result, -most), most).astype(held_as)


def setup_inputs(seed: int = 0) -> dict:
    seeds = jax.random.split(jax.random.key(seed), 4)
    u_wind = noise(seeds[0], (LEV, NLON, NLAT), 1.0, 6.0, ((1, 8), (2, 4)), jnp.float32)
    v_wind = noise(seeds[1], (LEV, NLON, NLAT), 1.0, 6.0, ((1, 8), (2, 4)), jnp.float32)
    height = noise(seeds[2], (LEV, NLON, NLAT), 1.0, 6.0, ((1, 8), (2, 4)), jnp.float32)
    return dict(u_wind=u_wind, v_wind=v_wind, height=height)


grav_zonal = 0.3
grav_merid = 0.6
coriolis = 0.8
divergence_coef = 0.3
diffusion = 0.08


def shifted(field, row_step, col_step, row_count, col_count):
    return field[:, 1 + row_step:1 + row_step + row_count, 1 + col_step:1 + col_step + col_count]


def stencil(padded, first_row, lat_total):
    row_count = padded.shape[2] - 2
    col_count = padded.shape[3] - 2
    height, u_wind, v_wind = padded[0], padded[1], padded[2]

    def view(field, row_step, col_step):
        return shifted(field, row_step, col_step, row_count, col_count)

    def laplace(field):
        return view(field, 0, 1) + view(field, 0, -1) + view(field, 1, 0) + view(field, -1, 0) - 4.0 * view(field, 0, 0)

    lat_index = (first_row + jnp.arange(row_count)).astype(jnp.float32)[:, None]
    center = (lat_index + 0.5) * (math.pi / lat_total)
    cos_center = jnp.sin(center)
    sin_center = -jnp.cos(center)
    face = (lat_index + 1.0) * (math.pi / lat_total)
    sin_face = -jnp.cos(face)
    cos_face = jnp.where(lat_index + 1.0 < lat_total, jnp.sin(face), 0.0)
    cos_south = jnp.sin(lat_index * (math.pi / lat_total))
    u_next = (view(u_wind, 0, 0) - grav_zonal * (view(height, 0, 1) - view(height, 0, 0)) / cos_center
              + coriolis * sin_center * 0.25 * (view(v_wind, 0, 0) + view(v_wind, 0, 1) + view(v_wind, -1, 0) + view(v_wind, -1, 1))
              + diffusion * laplace(u_wind))
    v_next = (view(v_wind, 0, 0) - grav_merid * (view(height, 1, 0) - view(height, 0, 0))
              - coriolis * sin_face * 0.25 * (view(u_wind, 0, 0) + view(u_wind, 0, -1) + view(u_wind, 1, 0) + view(u_wind, 1, -1))
              + diffusion * laplace(v_wind))
    flux = (view(u_wind, 0, 0) - view(u_wind, 0, -1)) + cos_face * view(v_wind, 0, 0) - cos_south * view(v_wind, -1, 0)
    height_next = view(height, 0, 0) - divergence_coef * flux / cos_center + diffusion * laplace(height)
    return jnp.stack([height_next, u_next, v_next])


def lon_pad(field):
    return jnp.concatenate([field[..., -1:], field, field[..., :1]], -1)


def polar_filter(field):
    lon_total = field.shape[-1]
    spectra = jnp.fft.rfft(field, axis=-1)
    wavenum = jnp.arange(lon_total // 2 + 1).astype(jnp.float32)
    sine_vals = jnp.sin(wavenum * (math.pi / lon_total))
    sine_sq = sine_vals * sine_vals
    lat_index = jnp.arange(NLAT).astype(jnp.float32)
    cosine = jnp.sin((lat_index + 0.5) * (math.pi / NLAT))
    damp_ratio = (2.0 * cosine * cosine)[:, None]
    damping = damp_ratio / jnp.maximum(sine_sq[None, :], damp_ratio)
    smoothed = jnp.fft.irfft(spectra * damping, n=lon_total, axis=-1).astype(field.dtype)
    row_index = jnp.arange(NLAT)
    is_polar = (row_index < NLAT // 4) | (row_index >= NLAT - NLAT // 4)
    return jnp.where(is_polar[:, None], smoothed, field)


def reference(u_wind, v_wind, height):
    u_wind = jnp.swapaxes(u_wind, 1, 2)
    v_wind = jnp.swapaxes(v_wind, 1, 2)
    height = jnp.swapaxes(height, 1, 2)
    half_lon = NLON // 2
    h_pad, u_pad, v_pad = lon_pad(height), lon_pad(u_wind), lon_pad(v_wind)
    h_turn = lon_pad(jnp.roll(height, -half_lon, axis=-1))
    u_turn = lon_pad(jnp.roll(u_wind, -half_lon, axis=-1))
    v_turn = lon_pad(jnp.roll(v_wind, -half_lon, axis=-1))
    h_ext = jnp.concatenate([h_turn[:, :1], h_pad, h_turn[:, -1:]], 1)
    u_ext = jnp.concatenate([-u_turn[:, :1], u_pad, -u_turn[:, -1:]], 1)
    v_ext = jnp.concatenate([jnp.zeros_like(v_pad[:, :1]), v_pad, -v_turn[:, -2:-1]], 1)
    stepped = stencil(jnp.stack([h_ext, u_ext, v_ext]), 0, NLAT)
    height_next = polar_filter(stepped[0])
    u_next = polar_filter(stepped[1])
    v_next = polar_filter(stepped[2])
    return jnp.swapaxes(u_next, 1, 2), jnp.swapaxes(v_next, 1, 2), jnp.swapaxes(height_next, 1, 2)
```

```python
import functools
import math

import jax
import jax.numpy as jnp
import numpy as np
from jax import lax
from jax.experimental import pallas as pl
from jax.experimental.pallas import tpu as pltpu
from jax.sharding import PartitionSpec as P

grav_zonal = 0.3
grav_merid = 0.6
coriolis = 0.8
divergence_coef = 0.3
diffusion = 0.08

F32 = jnp.float32
BF16 = jnp.bfloat16
RADIX = 8


def extended(block, rim):
    return jnp.concatenate([block, rim], axis=0)


def pack_kernel(levels, h_ref, u_ref, v_ref, rim_ref, edges_ref):
    level = pl.program_id(0)

    @pl.when(level == 0)
    def _():
        edges_ref[...] = jnp.zeros_like(edges_ref)

    lane = lax.broadcasted_iota(jnp.int32, edges_ref.shape, 1)
    last = edges_ref.shape[1] - 1
    edges = edges_ref[...]
    for field, ref in enumerate((h_ref, u_ref, v_ref)):
        whole = extended(ref[0], rim_ref[field, 0])
        low = whole[:, 0:1]
        high = whole[:, last : last + 1]
        edges = jnp.where(lane == field * levels + level, low, edges)
        edges = jnp.where(lane == (3 + field) * levels + level, high, edges)
        if field == 2:
            edges = jnp.where(lane == 6 * levels + level, whole[:, last - 1 : last], edges)
    edges_ref[...] = edges


def stencil_kernel(levels, h_ref, u_ref, v_ref, rim_ref, south_ref, north_ref, coef_ref, out_ref):
    level = pl.program_id(0)
    rows = h_ref.shape[1]
    shape = south_ref.shape
    lane = lax.broadcasted_iota(jnp.int32, shape, 1)
    width = shape[1]
    south_edges = south_ref[...]
    north_edges = north_ref[...]

    def east(x):
        return pltpu.roll(x, shape[0] - 1, 0)

    def west(x):
        return pltpu.roll(x, 1, 0)

    def south(x, field):
        edge = pltpu.roll(south_edges, lax.rem(width - (field * levels + level), width), 1)
        return jnp.where(lane == 0, edge, pltpu.roll(x, 1, 1))

    def north(x, field):
        edge = pltpu.roll(north_edges, width - 1 - (field * levels + level), 1)
        return jnp.where(lane == width - 1, edge, pltpu.roll(x, width - 1, 1))

    h = extended(h_ref[0], rim_ref[0, 0])
    u = extended(u_ref[0], rim_ref[1, 0])
    v = extended(v_ref[0], rim_ref[2, 0])
    inverse_cos = coef_ref[0:1]
    sin_center = coef_ref[1:2]
    sin_face = coef_ref[2:3]
    cos_face = coef_ref[3:4]
    cos_south = coef_ref[4:5]
    h_south, h_north = south(h, 0), north(h, 0)
    u_south, u_north = south(u, 1), north(u, 1)
    v_south, v_north = south(v, 2), north(v, 2)
    h_east, u_west = east(h), west(u)
    v_pair = v + v_south
    u_pair = u + u_north
    u_lap = east(u) + u_west + u_north + u_south - 4.0 * u
    v_lap = east(v) + west(v) + v_north + v_south - 4.0 * v
    h_lap = h_east + west(h) + h_north + h_south - 4.0 * h
    u_step = (
        u
        - (grav_zonal * inverse_cos) * (h_east - h)
        + (coriolis * 0.25 * sin_center) * (v_pair + east(v_pair))
        + diffusion * u_lap
    )
    v_step = (
        v
        - grav_merid * (h_north - h)
        - (coriolis * 0.25 * sin_face) * (u_pair + west(u_pair))
        + diffusion * v_lap
    )
    flux = u - u_west + cos_face * v - cos_south * v_south
    h_step = h - (divergence_coef * inverse_cos) * flux + diffusion * h_lap
    out_ref[0, 0] = h_step[:rows]
    out_ref[1, 0] = u_step[:rows]
    out_ref[2, 0] = v_step[:rows]


def split(x):
    high = x.astype(BF16)
    return high, (x - high.astype(F32)).astype(BF16)


def triple_dot(high, low, x):
    x_high, x_low = split(x)
    return (
        jnp.dot(high, x_high, preferred_element_type=F32)
        + jnp.dot(high, x_low, preferred_element_type=F32)
        + jnp.dot(low, x_high, preferred_element_type=F32)
    )


def forward_parts(x):
    half = math.sqrt(0.5)
    a = [x[p] + x[p + 4] for p in range(4)]
    b = [x[p] - x[p + 4] for p in range(4)]
    even, odd = a[0] + a[2], a[1] + a[3]
    minus, plus = half * (b[1] - b[3]), half * (b[1] + b[3])
    return [
        (even + odd,),
        (b[0] + minus, -(b[2] + plus)),
        (a[0] - a[2], a[3] - a[1]),
        (b[0] - minus, b[2] - plus),
        (even - odd,),
    ]


def inverse_parts(z):
    half = math.sqrt(0.5)
    z0, z4 = z[0][0], z[4][0]
    (r1, i1), (r2, i2), (r3, i3) = z[1], z[2], z[3]
    even_p, even_m = z0 + z4 + r2, z0 + z4 - r2
    odd_p, odd_m = z0 - z4 - i2, z0 - z4 + i2
    c0 = r1 + r3
    c1 = half * (r1 - i1 - r3 - i3)
    c2 = i3 - i1
    c3 = half * (r3 - i3 - r1 - i1)
    base = [even_p, odd_p, even_m, odd_m]
    waves = [c0, c1, c2, c3]
    return [base[p] + waves[p] for p in range(4)] + [base[p] - waves[p] for p in range(4)]


def filter_kernel(x_ref, fh_ref, fl_ref, gh_ref, gl_ref, eh_ref, el_ref, ih_ref, il_ref, damp_ref, out_ref):
    n_lon, pair, cols, width = x_ref.shape
    group = n_lon // RADIX
    span = group * cols
    blocks = [
        jnp.concatenate(
            [
                jnp.concatenate([x_ref[p * group + j, item] for item in range(pair)], axis=1)
                for j in range(group)
            ],
            axis=0,
        )
        for p in range(RADIX)
    ]
    parts = forward_parts(blocks)
    waves = []
    first = 0
    for kind in range(5):
        if kind in (0, 4):
            slot = kind // 4
            y = parts[kind][0]
            count = span
            fh, fl, gh, gl = eh_ref[slot], el_ref[slot], ih_ref[slot], il_ref[slot]
        else:
            slot = kind - 1
            y = jnp.concatenate(parts[kind], axis=0)
            count = 2 * span
            fh, fl, gh, gl = fh_ref[slot], fl_ref[slot], gh_ref[slot], gl_ref[slot]
        damp = damp_ref[first : first + count]
        first += count
        spectrum = triple_dot(fh, fl, y) * jnp.concatenate([damp] * pair, axis=1)
        z = triple_dot(gh, gl, spectrum)
        waves.append((z,) if count == span else (z[:span], z[span:]))
    for p, block in enumerate(inverse_parts(waves)):
        for j in range(group):
            for item in range(pair):
                out_ref[p * group + j, item] = block[
                    j * cols : (j + 1) * cols, item * width : (item + 1) * width
                ]


def fourier_tables(lon_total):
    span = lon_total // RADIX
    q = np.arange(span)
    real_tables, complex_tables = [], []
    wavenums, weights = [], []
    for kind in range(5):
        if kind == 0:
            k_cos = RADIX * np.arange(span // 2 + 1)
            k_sin = RADIX * np.arange(1, span // 2)
        elif kind == 4:
            k_cos = k_sin = RADIX * np.arange(span // 2) + 4
        else:
            k_cos = k_sin = RADIX * np.arange(span) + kind
        cos_rows = np.cos((k_cos[:, None] * q % lon_total) * (2.0 * math.pi / lon_total))
        sin_rows = np.sin((k_sin[:, None] * q % lon_total) * (2.0 * math.pi / lon_total))
        if kind in (0, 4):
            real_tables.append(np.concatenate([cos_rows, sin_rows], 0))
        else:
            complex_tables.append(np.block([[cos_rows, sin_rows], [-sin_rows, cos_rows]]))
        k_all = np.concatenate([k_cos, k_sin])
        wavenums.append(k_all)
        weights.append(np.where((k_all == 0) | (k_all == lon_total // 2), 1.0, 2.0) / lon_total)
    wavenums = np.concatenate(wavenums)
    sine_sq = np.sin(wavenums * (math.pi / lon_total)) ** 2

    def halves(tables):
        table = np.stack(tables).astype(np.float32)
        high = table.astype(jnp.bfloat16)
        low = (table - high.astype(np.float32)).astype(jnp.bfloat16)
        turn = lambda t: np.ascontiguousarray(np.swapaxes(t, 1, 2))
        return high, low, turn(high), turn(low)

    return halves(complex_tables), halves(real_tables), sine_sq, np.concatenate(weights)


def latitude_table(rows, lat_total):
    g = np.arange(lat_total)
    cos_center = np.sin((g + 0.5) * math.pi / lat_total)
    table = np.zeros((8, lat_total))
    table[0] = 1.0 / cos_center
    table[1] = -np.cos((g + 0.5) * math.pi / lat_total)
    table[2] = -np.cos((g + 1.0) * math.pi / lat_total)
    table[3] = np.where(g + 1 < lat_total, np.sin((g + 1.0) * math.pi / lat_total), 0.0)
    table[4] = np.sin(g * math.pi / lat_total)
    table[5] = 2.0 * cos_center * cos_center
    return table.reshape(8, lat_total // rows, rows).swapaxes(0, 1).astype(np.float32)


def ring(axis, step, wrap=True):
    size = lax.axis_size(axis)
    return [(i, (i + step) % size) for i in range(size) if wrap or 0 <= i + step < size]


def shards(u_wind, v_wind, height):
    levels, cols, rows = height.shape
    n_lat, n_lon = lax.axis_size("lat"), lax.axis_size("lon")
    lat_total, lon_total = rows * n_lat, cols * n_lon
    band = lax.axis_index("lat")
    fields = (height, u_wind, v_wind)
    ext = -(-(cols + 2) // 8) * 8
    spare = ext - cols

    lasts = jnp.stack([f[:, cols - 1] for f in fields])
    firsts = jnp.stack([f[:, 0] for f in fields])
    west_rim = lax.ppermute(lasts, "lon", ring("lon", 1))
    east_rim = lax.ppermute(firsts, "lon", ring("lon", -1))
    middle = jnp.zeros((3, levels, spare - 2, rows), F32)
    rim = jnp.concatenate([east_rim[:, :, None], middle, west_rim[:, :, None]], 2)

    level_spec = pl.BlockSpec((1, cols, rows), lambda l: (l, 0, 0))
    rim_spec = pl.BlockSpec((3, 1, spare, rows), lambda l: (0, l, 0, 0))
    edge_spec = pl.BlockSpec((ext, rows), lambda l: (0, 0))
    edges = pl.pallas_call(
        functools.partial(pack_kernel, levels),
        grid=(levels,),
        in_specs=[level_spec] * 3 + [rim_spec],
        out_specs=edge_spec,
        out_shape=jax.ShapeDtypeStruct((ext, rows), F32),
        compiler_params=pltpu.CompilerParams(vmem_limit_bytes=32 * 1024 * 1024),
    )(*fields, rim)

    from_south = lax.ppermute(edges, "lat", ring("lat", 1, False))
    from_north = lax.ppermute(edges, "lat", ring("lat", -1, False))
    across = lax.ppermute(edges, "lon", ring("lon", n_lon // 2))
    count = levels
    pad = jnp.zeros((ext, rows - 3 * count), F32)
    south_wall = jnp.concatenate(
        [across[:, :count], -across[:, count : 2 * count], jnp.zeros((ext, count), F32)], 1
    )
    north_wall = jnp.concatenate(
        [
            across[:, 3 * count : 4 * count],
            -across[:, 4 * count : 5 * count],
            -across[:, 6 * count : 7 * count],
        ],
        1,
    )
    south_edges = jnp.where(band == 0, south_wall, from_south[:, 3 * count : 6 * count])
    north_edges = jnp.where(band == n_lat - 1, north_wall, from_north[:, : 3 * count])
    south_edges = jnp.concatenate([south_edges, pad], 1)
    north_edges = jnp.concatenate([north_edges, pad], 1)

    coef = lax.dynamic_index_in_dim(jnp.asarray(latitude_table(rows, lat_total)), band, 0, False)
    stepped = pl.pallas_call(
        functools.partial(stencil_kernel, levels),
        grid=(levels,),
        in_specs=[level_spec] * 3
        + [rim_spec, edge_spec, edge_spec, pl.BlockSpec((8, rows), lambda l: (0, 0))],
        out_specs=pl.BlockSpec((3, 1, cols, rows), lambda l: (0, l, 0, 0)),
        out_shape=jax.ShapeDtypeStruct((3, levels, cols, rows), F32),
        compiler_params=pltpu.CompilerParams(vmem_limit_bytes=40 * 1024 * 1024),
    )(*fields, rim, south_edges, north_edges, coef)

    items = 3 * levels // n_lon
    pair = 2 if items % 2 == 0 else 1
    arrived = lax.all_to_all(
        stepped.reshape(n_lon, items, cols, rows), "lon", split_axis=0, concat_axis=0
    )
    complex_tables, real_tables, sine_sq, weight = fourier_tables(lon_total)
    ratio = coef[5][None, :]
    damp = (
        jnp.asarray(weight, F32)[:, None]
        * ratio
        / jnp.maximum(jnp.asarray(sine_sq, F32)[:, None], ratio)
    )
    item_spec = pl.BlockSpec((n_lon, pair, cols, rows), lambda i: (0, i, 0, 0))
    whole = pl.BlockSpec(memory_space=pltpu.VMEM)
    smoothed = pl.pallas_call(
        filter_kernel,
        grid=(items // pair,),
        in_specs=[item_spec] + [whole] * 9,
        out_specs=item_spec,
        out_shape=jax.ShapeDtypeStruct((n_lon, items, cols, rows), F32),
        compiler_params=pltpu.CompilerParams(vmem_limit_bytes=56 * 1024 * 1024),
    )(
        arrived,
        *(jnp.asarray(t) for t in complex_tables),
        *(jnp.asarray(t) for t in real_tables),
        damp,
    )
    returned = lax.all_to_all(smoothed, "lon", split_axis=0, concat_axis=0)
    returned = returned.reshape(3, levels, cols, rows)
    is_polar = (band < n_lat // 4) | (band >= n_lat - n_lat // 4)
    result = [jnp.where(is_polar, returned[f], stepped[f]) for f in range(3)]
    return result[1], result[2], result[0]


def solution(mesh):
    placed = (P(None, "lon", "lat"),) * 3
    return jax.shard_map(shards, mesh=mesh, in_specs=placed, out_specs=placed, check_vma=False)
```
